512 devices in a mesh: section: 2 (over core), dp: 32 (over x, y), mp: 8 (over z).
Axes of the slice: x: 4, y: 8, z: 8, core: 2. Of those that a mesh axis runs over, the one named last changes fastest.
Arguments:
- rollout_rows: bfloat16 [2, 32, 8, 8192], P('section', 'dp', None, 'mp'), may hold values from -6 to 6
- response_lengths: int32 [2, 32], P('section', 'dp'), may hold values from 1 to 4, 80 in all within a row
- tile_counts: int32 [2, 32], P('section', 'dp'), may hold values from 1 to 2, 48 in all within a row
- prompt_owner: int32 [2, 32], P('section'), may hold values from 0 to 31, each once within a row
- proj_gain: bfloat16 [8192], P('mp'), may hold values from 0.099609375 to 1.8984375
- proj_in: bfloat16 [8192, 8192], P('mp', 'dp'), may hold values from -0.0625 to 0.0625
- proj_out: bfloat16 [8192, 8192], P('dp', 'mp'), may hold values from -0.0625 to 0.0625
- norm_gain: bfloat16 [2, 8192], P('section', 'mp'), may hold values from 0.099609375 to 1.8984375
- gate_w: bfloat16 [2, 8192, 16384], P('section', 'mp', 'dp'), may hold values from -0.0625 to 0.0625
- up_w: bfloat16 [2, 8192, 16384], P('section', 'mp', 'dp'), may hold values from -0.0625 to 0.0625
- down_w: bfloat16 [2, 16384, 8192], P('section', 'dp', 'mp'), may hold values from -0.046875 to 0.046875
Outputs:
- section_hidden: bfloat16 [2, 2, 256, 8192], P('section', None, 'dp', 'mp')
The draws below stay inside these ranges and needn't reach their ends.
Inputs may be any that keep to these rules, and one draw needn't show every extreme that they name: In each micro-batch every owner slot gets exactly one prompt; prompt k of micro-batch m goes to owner slot prompt_owner[m, k], which is held by dp device prompt_owner[m, k]; each dp device owns exactly one slot.
All inputs are finite; a program needn't handle non-finite values. No bound on the sum of `response_lengths` or of `tile_counts` on one device may be relied on, other than what follows from the above.
Results may differ from the reference program's by a relative error of at most 0.03.
Values may be sent and summed in bfloat16 or wider, within the bound.
No kernel may reach another device: no remote copies, remote signals or barrier semaphores. Data moves between devices by JAX's collectives and lax.ppermute only.
A program may use at most 64 MiB of HBM per device.

```python
import math
import jax
import jax.numpy as jnp
import numpy as np
from jax import lax

D = 8192
VIS = 8192
FF = 16384
MAXT = 2
TROWS = 2
LMAX = 4
SLOT = 8
PROMPTS_ALL = 32


def levels(own_key, dims, cuts, least, top_value):
    factor_of, own = 1.0, jax.random.fold_in(own_key, 6)
    for axis_at, shards_of in cuts:
        heights = jnp.exp(jax.random.uniform(jax.random.fold_in(own, axis_at), (shards_of,), jnp.float32, least / len(cuts), top_value / len(cuts)))
        factor_of = factor_of * jnp.repeat(heights, dims[axis_at] // shards_of).reshape([-1 if axis == axis_at else 1 for axis in range(len(dims))])
    return factor_of


def split_up(count, total, limit, skew):
    weights = [(1 << 20) // math.isqrt(standing ** skew) + 1 for standing in range(2, count + 1)]
    rest, given = total - limit - (count - 1), [1] * (count - 1)
    while rest > 0:
        free = [i for i in range(count - 1) if given[i] < limit]
        whole, remaining = sum([weights[i] for i in free]), rest
        for i in free:
            addition = min(limit - given[i], max(1, remaining * weights[i] // whole), rest)
            given[i] = given[i] + addition
            rest = rest - addition
    return np.array([limit] + given)


def uneven(own_key, number_of, total, most, slope):
    if number_of == 2:
        one = jax.random.randint(own_key, (), max(1, total - most), min(most, total - 1) + 1)
        return jnp.stack([one, total - one])
    sizes = jnp.asarray(split_up(number_of, total, most, slope), jnp.int32)
    pairs = (number_of - 1) // 2
    giver, taker = sizes[1:1 + 2 * pairs:2], sizes[2:2 + 2 * pairs:2]
    margin = jnp.minimum(giver - 1, most - taker)
    moved = jax.random.randint(jax.random.fold_in(own_key, 1), (pairs,), 0, 1 << 20) % (margin + 1)
    sizes = sizes.at[1:1 + 2 * pairs:2].set(giver - moved).at[2:2 + 2 * pairs:2].set(taker + moved)
    return sizes[jax.random.permutation(jax.random.fold_in(own_key, 2), number_of)]


def bell_draw(own_key, shape, width, limit, cuts=(), kind=jnp.bfloat16):
    array = width * jax.random.normal(own_key, shape, jnp.float32)
    if cuts:
        array = array * levels(own_key, shape, cuts, -0.22, 0.18)
    return jnp.clip(array, -limit, limit).astype(kind)


def setup_inputs(seed: int = 0) -> dict:
    key_of = jax.random.split(jax.random.key(seed), 12)
    rollout_rows = bell_draw(key_of[0], (2, PROMPTS_ALL, SLOT, D), 1.0, 6.0, ((0, 2), (1, 32), (3, 8)))
    response_lengths = jax.vmap(lambda own: uneven(own, PROMPTS_ALL, PROMPTS_ALL * 5 * LMAX // 8, LMAX, 1))(jax.random.split(key_of[1], 2)).reshape((2, PROMPTS_ALL)).astype(jnp.int32)
    tile_counts = jax.vmap(lambda own: uneven(own, PROMPTS_ALL, PROMPTS_ALL * 3 * MAXT // 4, MAXT, 0))(jax.random.split(key_of[2], 2)).reshape((2, PROMPTS_ALL)).astype(jnp.int32)
    prompt_owner = jax.vmap(lambda own: jax.random.permutation(own, PROMPTS_ALL))(jax.random.split(key_of[3], 2)).reshape((2, PROMPTS_ALL)).astype(jnp.int32)
    proj_gain = jnp.clip(1.0 + 0.18 * jax.random.normal(key_of[4], (VIS,), jnp.float32), 0.099609375, 1.8984375).astype(jnp.bfloat16)
    proj_in = bell_draw(key_of[5], (VIS, D), VIS ** -0.5, 0.0625, ((0, 8), (1, 32)))
    proj_out = bell_draw(key_of[6], (D, D), D ** -0.5, 0.0625, ((0, 32), (1, 8)))
    norm_gain = jnp.clip(1.0 + 0.18 * jax.random.normal(key_of[7], (2, D), jnp.float32), 0.099609375, 1.8984375).astype(jnp.bfloat16)
    gate_w = bell_draw(key_of[8], (2, D, FF), D ** -0.5, 0.0625, ((0, 2), (1, 8), (2, 32)))
    up_w = bell_draw(key_of[9], (2, D, FF), D ** -0.5, 0.0625, ((0, 2), (1, 8), (2, 32)))
    down_w = bell_draw(key_of[10], (2, FF, D), FF ** -0.5, 0.046875, ((0, 2), (1, 32), (2, 8)))
    return dict(rollout_rows=rollout_rows, response_lengths=response_lengths, tile_counts=tile_counts, prompt_owner=prompt_owner, proj_gain=proj_gain, proj_in=proj_in, proj_out=proj_out, norm_gain=norm_gain, gate_w=gate_w, up_w=up_w, down_w=down_w)


EPS_LN = 1e-05
EPS_RMS = 1e-06

def keep_live(slot_rows, lengths, tile_count):
    image_rows = MAXT * TROWS
    position = jnp.arange(slot_rows.shape[1], dtype=jnp.int32)[None, :]
    keeping = jnp.where(position < image_rows, position < tile_count[:, None] * TROWS, position - image_rows < lengths[:, None])
    return slot_rows * keeping[:, :, None].astype(slot_rows.dtype)

def project(image, gain, w_in, w_out):
    values = image.astype(jnp.float32)
    center = lax.optimization_barrier(jnp.mean(values, axis=1))
    spread = lax.optimization_barrier(jnp.mean(values * values, axis=1)) - center * center
    scaled = (values * gain.astype(jnp.float32)).astype(jnp.bfloat16)
    mixture = jnp.dot(scaled, w_in, preferred_element_type=jnp.float32)
    column = jnp.dot(gain[None, :], w_in, preferred_element_type=jnp.float32)
    before = (mixture - center[:, None] * column) * lax.rsqrt(spread + EPS_LN)[:, None]
    active = jax.nn.gelu(before, approximate=False).astype(jnp.bfloat16)
    return jnp.dot(active, w_out, preferred_element_type=jnp.float32).astype(jnp.bfloat16)

def section_layer(sequence, gain, w_gate, w_up, w_down):
    values = sequence.astype(jnp.float32)
    squares = lax.optimization_barrier(jnp.mean(values * values, axis=1))
    factor = lax.rsqrt(squares + EPS_RMS)[:, None]
    normed = (values * gain.astype(jnp.float32)).astype(jnp.bfloat16)
    gate_pre = jnp.dot(normed, w_gate, preferred_element_type=jnp.float32) * factor
    up_pre = jnp.dot(normed, w_up, preferred_element_type=jnp.float32) * factor
    inner = (jax.nn.silu(gate_pre) * up_pre).astype(jnp.bfloat16)
    return (values + jnp.dot(inner, w_down, preferred_element_type=jnp.float32)).astype(jnp.bfloat16)

def reference(rollout_rows, response_lengths, tile_counts, prompt_owner, proj_gain, proj_in, proj_out, norm_gain, gate_w, up_w, down_w):
    image_rows = MAXT * TROWS
    early_list = []
    late_list = []
    for member in range(2):
        live = keep_live(rollout_rows[member], response_lengths[member], tile_counts[member])
        total = live.shape[0]
        source = jnp.zeros((total,), jnp.int32).at[prompt_owner[member]].set(jnp.arange(total, dtype=jnp.int32))
        ordered = live[source]
        image = ordered[:, :image_rows].reshape(total * image_rows, VIS)
        projected = project(image, proj_gain, proj_in, proj_out).reshape(total, image_rows, D)
        sequence = jnp.concatenate([projected, ordered[:, image_rows:]], axis=1).reshape(total * (image_rows + LMAX), D)
        first_out = section_layer(sequence, norm_gain[0], gate_w[0], up_w[0], down_w[0])
        second_out = section_layer(first_out, norm_gain[1], gate_w[1], up_w[1], down_w[1])
        early_list.append(first_out)
        late_list.append(second_out)
    return jnp.stack([jnp.stack(early_list), jnp.stack(late_list)])
```

```python
import jax
import jax.numpy as jnp
from jax import lax
from jax.sharding import PartitionSpec as P

D = 8192
VIS = 8192
MAXT = 2
TROWS = 2
LMAX = 4
IMG = MAXT * TROWS
SLOT = IMG + LMAX
EPS_LN = 1e-05
EPS_RMS = 1e-06
LANES = 128
BF = jnp.bfloat16
F32 = jnp.float32


def exchange(blocks, axis):
    return lax.all_to_all(blocks, axis, 0, 0, tiled=True)


def spread(block, axis):
    peers = lax.axis_size(axis)
    return exchange(jnp.broadcast_to(block[None], (peers,) + block.shape), axis)


def swap(block):
    return lax.ppermute(block, "section", [(0, 1), (1, 0)])


def terms(values, count):
    parts = []
    for _ in range(count):
        part = lax.reduce_precision(values, 8, 7)
        parts.append(part.astype(BF))
        values = values - part
    return parts


def dot(a, b):
    return jnp.dot(a, b, preferred_element_type=F32)


def keep_live(slot_rows, lengths, tile_count):
    position = jnp.arange(slot_rows.shape[1], dtype=jnp.int32)[None, :]
    keeping = jnp.where(
        position < IMG,
        position < tile_count[:, None] * TROWS,
        position - IMG < lengths[:, None],
    )
    return slot_rows * keeping[:, :, None].astype(slot_rows.dtype)


def projector_partial(image, gain, w_in):
    width = image.shape[1]
    values = image.astype(F32)
    sums = jnp.sum(values, axis=1)
    squares = jnp.sum(values * values, axis=1)
    scaled = (values * gain.astype(F32)).astype(BF)
    column = dot(gain[None, :], w_in)
    centered = dot(scaled, w_in) - (sums / width)[:, None] * column
    rows, hidden = centered.shape
    small = jnp.stack(terms(sums, 3) + terms(squares, 3))
    small = jnp.pad(small, ((0, 0), (0, hidden - rows)))
    extra = jnp.concatenate([small, jnp.concatenate(terms(column, 3))], axis=0)
    extra = jnp.pad(extra, ((0, 16 - extra.shape[0]), (0, 0)))
    return jnp.concatenate([centered.astype(BF), extra], axis=0)


def projector_active(parts, rows, width):
    values = parts.astype(F32)
    extra = values[:, rows:]
    sums = jnp.sum(extra[:, 0:3, :rows], axis=1)
    squares = jnp.sum(extra[:, 3:6, :rows], axis=(0, 1))
    columns = jnp.sum(extra[:, 6:9], axis=1)
    center = jnp.sum(sums, axis=0) / VIS
    variance = squares / VIS - center * center
    offsets = sums / width - center[None, :]
    before = jnp.sum(values[:, :rows], axis=0)
    before = before + jnp.sum(offsets[:, :, None] * columns[:, None, :], axis=0)
    before = before * lax.rsqrt(variance + EPS_LN)[:, None]
    return jax.nn.gelu(before, approximate=False).astype(BF)


def layer_partial(rows, gain, w_gate, w_up):
    values = rows.astype(F32)
    squares = jnp.sum(values * values, axis=1)
    normed = (values * gain.astype(F32)).astype(BF)
    stats = jnp.pad(jnp.stack(terms(squares, 2), axis=1), ((0, 0), (0, LANES - 2)))
    return jnp.concatenate(
        [dot(normed, w_gate).astype(BF), dot(normed, w_up).astype(BF), stats], axis=1
    )


def layer_inner(parts, hidden):
    total = jnp.sum(parts.astype(F32), axis=0)
    squares = jnp.sum(total[:, 2 * hidden :], axis=1)
    factor = lax.rsqrt(squares / D + EPS_RMS)[:, None]
    gate_pre = total[:, :hidden] * factor
    up_pre = total[:, hidden : 2 * hidden] * factor
    return (jax.nn.silu(gate_pre) * up_pre).astype(BF)


def layer_blocks(rows, gain, w_gate, w_up, w_down, ordering):
    mp = lax.axis_size("mp")
    dp = lax.axis_size("dp")
    hidden = w_gate.shape[1]
    sent = layer_partial(rows, gain, w_gate, w_up)
    parts = exchange(sent.reshape(mp, rows.shape[0] // mp, -1), "mp")
    inner = spread(layer_inner(parts, hidden), "mp").reshape(rows.shape[0], hidden)
    if ordering is not None:
        inner = dot(ordering, inner).astype(BF)
    blocks = dot(inner, w_down).astype(BF)
    blocks = exchange(blocks.reshape(dp, -1, blocks.shape[1]), "dp")
    return jnp.sum(blocks.astype(F32), axis=0)


def per_device(
    rollout_rows,
    response_lengths,
    tile_counts,
    prompt_owner,
    proj_gain,
    proj_in,
    proj_out,
    norm_gain,
    gate_w,
    up_w,
    down_w,
):
    dp = lax.axis_size("dp")
    width = rollout_rows.shape[3]
    first = lax.axis_index("section") == 0
    place = lax.axis_index("dp")
    owners = prompt_owner[0]
    own = (norm_gain, gate_w[0], up_w[0], down_w[0])
    other = tuple(swap(array) for array in own)
    layer0 = [jnp.where(first, a, b) for a, b in zip(own, other)]
    layer1 = [jnp.where(first, b, a) for a, b in zip(own, other)]
    layer0[0], layer1[0] = layer0[0][0], layer1[0][0]

    live = keep_live(rollout_rows[0], response_lengths[0], tile_counts[0])[0]
    gathered = spread(live, "dp")
    image = gathered[:, :IMG].reshape(dp * IMG, width)

    sent = projector_partial(image, proj_gain, proj_in)
    parts = spread(sent, "mp")
    active = projector_active(parts, dp * IMG, width)
    blocks = exchange(dot(active, proj_out).astype(BF).reshape(dp, IMG, width), "dp")
    projected = jnp.sum(blocks.astype(F32), axis=0).astype(BF)
    all_projected = spread(projected, "dp")

    own_rows = jnp.concatenate([projected, live[IMG:]], axis=0)
    rows = jnp.concatenate([all_projected, gathered[:, IMG:]], axis=1).reshape(dp * SLOT, width)
    total = layer_blocks(rows, *layer0, None)
    own_next = (own_rows.astype(F32) + total).astype(BF)
    rows_next = spread(own_next, "dp")

    source = jnp.sum(jnp.where(owners == place, jnp.arange(dp, dtype=jnp.int32), 0))
    slot_early = lax.dynamic_index_in_dim(rows_next, source, 0, keepdims=False)
    row_at = jnp.arange(dp * SLOT, dtype=jnp.int32)
    target = (owners[:, None] * SLOT + jnp.arange(SLOT, dtype=jnp.int32)[None, :]).reshape(-1)
    ordering = (row_at[:, None] == target[None, :]).astype(BF)
    total = layer_blocks(rows_next.reshape(dp * SLOT, width), *layer1, ordering)
    slot_late = (slot_early.astype(F32) + total).astype(BF)

    came = swap(jnp.where(first, slot_late, slot_early))
    kept = jnp.where(first, slot_early, slot_late)
    return jnp.where(first, jnp.stack([kept, came]), jnp.stack([came, kept]))[None]


def solution(mesh):
    placed = (
        P("section", "dp", None, "mp"),
        P("section", "dp"),
        P("section", "dp"),
        P("section", None),
        P("mp"),
        P("mp", "dp"),
        P("dp", "mp"),
        P("section", "mp"),
        P("section", "mp", "dp"),
        P("section", "mp", "dp"),
        P("section", "dp", "mp"),
    )
    return jax.shard_map(
        per_device,
        mesh=mesh,
        in_specs=placed,
        out_specs=P("section", None, "dp", "mp"),
        check_vma=False,
    )
```

```python
import jax
import jax.numpy as jnp
from jax import lax
from jax.sharding import PartitionSpec as P

D = 8192
VIS = 8192
MAXT = 2
TROWS = 2
LMAX = 4
IMG = MAXT * TROWS
SLOT = IMG + LMAX
EPS_LN = 1e-05
EPS_RMS = 1e-06
LANES = 128
DEAD = 64.0
BF = jnp.bfloat16
F32 = jnp.float32


def exchange(blocks, axis):
    return lax.all_to_all(blocks, axis, 0, 0, tiled=True)


def spread(block, axis):
    peers = lax.axis_size(axis)
    return exchange(jnp.broadcast_to(block[None], (peers,) + block.shape), axis)


def swap(block):
    return lax.ppermute(block, "section", [(0, 1), (1, 0)])


def terms(values, count):
    parts = []
    for _ in range(count):
        part = lax.reduce_precision(values, 8, 7)
        parts.append(part.astype(BF))
        values = values - part
    return parts


def dot(a, b):
    return jnp.dot(a, b, preferred_element_type=F32)


def doubling_gather(block, axis):
    peers = lax.axis_size(axis)
    blocks = block[None]
    while blocks.shape[0] < peers:
        step = blocks.shape[0]
        came = lax.ppermute(blocks, axis, [(i, i ^ step) for i in range(peers)])
        blocks = jnp.concatenate([blocks, came], axis=0)
    return blocks


def marked(rows, count):
    alive = jnp.arange(rows.shape[0], dtype=jnp.int32) < count
    return jnp.where(alive[:, None], rows, jnp.asarray(DEAD, rows.dtype))


def placement(rows, key, kept):
    count = rows.shape[0]
    alive = jnp.broadcast_to((rows[:, :1] < DEAD / 2), (count, LANES)).astype(BF)
    before = (key[None, :] < key[:, None]).astype(BF)
    position = dot(before, alive)[:, :kept]
    at = lax.broadcasted_iota(jnp.int32, (count, kept), 1).astype(F32)
    return jnp.where(position == at, alive[:, :kept], jnp.asarray(0, BF))


def pick(matrix, rows):
    return lax.dot_general(
        matrix, rows, (((0,), (0,)), ((), ())), preferred_element_type=F32
    ).astype(BF)


def to_tiles(rows):
    count, width = rows.shape
    tiles = rows.reshape(count // 8, 8, width // LANES, LANES).transpose(0, 2, 1, 3)
    return tiles.reshape(-1, LANES)


def from_tiles(tiles, width):
    columns = width // LANES
    rows = tiles.reshape(-1, columns, 8, LANES).transpose(0, 2, 1, 3)
    return rows.reshape(-1, width)


def projector_partial(image, gain, w_in):
    width = image.shape[1]
    values = image.astype(F32)
    sums = jnp.sum(values, axis=1)
    squares = jnp.sum(values * values, axis=1)
    scaled = (values * gain.astype(F32)).astype(BF)
    column = dot(gain[None, :], w_in)
    centered = dot(scaled, w_in) - (sums / width)[:, None] * column
    rows, hidden = centered.shape
    small = jnp.stack(terms(sums, 3) + terms(squares, 3))
    small = jnp.pad(small, ((0, 0), (0, hidden - rows)))
    extra = jnp.concatenate([small, jnp.concatenate(terms(column, 3))], axis=0)
    extra = jnp.pad(extra, ((0, 16 - extra.shape[0]), (0, 0)))
    return jnp.concatenate([centered.astype(BF), extra], axis=0)


def projector_active(parts, rows, width):
    values = parts.astype(F32)
    extra = values[:, rows:]
    sums = jnp.sum(extra[:, 0:3, :rows], axis=1)
    squares = jnp.sum(extra[:, 3:6, :rows], axis=(0, 1))
    columns = jnp.sum(extra[:, 6:9], axis=1)
    center = jnp.sum(sums, axis=0) / VIS
    variance = squares / VIS - center * center
    offsets = sums / width - center[None, :]
    before = jnp.sum(values[:, :rows], axis=0)
    before = before + jnp.sum(offsets[:, :, None] * columns[:, None, :], axis=0)
    before = before * lax.rsqrt(variance + EPS_LN)[:, None]
    return jax.nn.gelu(before, approximate=False).astype(BF)


def layer_partial(rows, gain, w_gate, w_up):
    values = rows.astype(F32)
    squares = jnp.sum(values * values, axis=1)
    normed = (values * gain.astype(F32)).astype(BF)
    stats = jnp.pad(jnp.stack(terms(squares, 2), axis=1), ((0, 0), (0, LANES - 2)))
    return jnp.concatenate(
        [dot(normed, w_gate).astype(BF), dot(normed, w_up).astype(BF), stats], axis=1
    )


def layer_inner(parts, hidden):
    total = jnp.sum(parts.astype(F32), axis=0)
    squares = jnp.sum(total[:, 2 * hidden :], axis=1)
    factor = lax.rsqrt(squares / D + EPS_RMS)[:, None]
    gate_pre = total[:, :hidden] * factor
    up_pre = total[:, hidden : 2 * hidden] * factor
    return (jax.nn.silu(gate_pre) * up_pre).astype(BF)


def layer_hidden(rows, gain, w_gate, w_up):
    mp = lax.axis_size("mp")
    hidden = w_gate.shape[1]
    sent = layer_partial(rows, gain, w_gate, w_up)
    parts = exchange(sent.reshape(mp, rows.shape[0] // mp, -1), "mp")
    return spread(layer_inner(parts, hidden), "mp").reshape(rows.shape[0], hidden)


def summed(blocks):
    return jnp.sum(exchange(blocks, "dp").astype(F32), axis=0)


def per_device(
    rollout_rows,
    response_lengths,
    tile_counts,
    prompt_owner,
    proj_gain,
    proj_in,
    proj_out,
    norm_gain,
    gate_w,
    up_w,
    down_w,
):
    dp = lax.axis_size("dp")
    width = rollout_rows.shape[3]
    first = lax.axis_index("section") == 0
    place = lax.axis_index("dp")
    owners = prompt_owner[0]
    img_live = dp * TROWS * MAXT * 3 // 4
    own = (norm_gain, gate_w[0], up_w[0], down_w[0])
    other = tuple(swap(array) for array in own)
    layer0 = [jnp.where(first, a, b) for a, b in zip(own, other)]
    layer1 = [jnp.where(first, b, a) for a, b in zip(own, other)]
    layer0, layer1 = lax.optimization_barrier((layer0, layer1))
    layer0[0], layer1[0] = layer0[0][0], layer1[0][0]

    local = rollout_rows[0, 0]
    gathered = spread(marked(local[:IMG], tile_counts[0, 0] * TROWS), "dp")
    gathered = gathered.reshape(dp * IMG, width)
    replies = doubling_gather(marked(local[IMG:], response_lengths[0, 0]), "dp")
    replies = replies.reshape(dp * LMAX, width)

    index = jnp.arange(dp * IMG, dtype=jnp.int32)
    place_image = placement(gathered, index, img_live)
    image = pick(place_image, gathered)
    sent = projector_partial(image, proj_gain, proj_in)
    parts = spread(sent, "mp")
    active = projector_active(parts, img_live, width)
    blocks = to_tiles(dot(active, proj_out).astype(BF))
    projected = summed(blocks.reshape(dp, -1, LANES)).astype(BF)
    projected = from_tiles(spread(projected, "dp"), width)

    prompt_at = (index // LMAX) ^ place
    place_reply = placement(replies, prompt_at * LMAX + index % LMAX, img_live)
    rows = jnp.concatenate([projected, pick(place_reply, replies)], axis=0)

    slot_row = jnp.arange(dp * SLOT, dtype=jnp.int32)
    image_row = owners[:, None] * SLOT + jnp.arange(IMG, dtype=jnp.int32)[None, :]
    all_prompts = jnp.arange(dp, dtype=jnp.int32)
    met = (all_prompts[:, None] ^ place) == all_prompts[None, :]
    met_owner = jnp.sum(jnp.where(met, owners[None, :], 0), axis=1)
    reply_row = met_owner[:, None] * SLOT + IMG + jnp.arange(LMAX, dtype=jnp.int32)[None, :]
    to_image = (slot_row[:, None] == image_row.reshape(-1)[None, :]).astype(BF)
    to_reply = (slot_row[:, None] == reply_row.reshape(-1)[None, :]).astype(BF)
    ordering = jnp.concatenate(
        [dot(to_image, place_image).astype(BF), dot(to_reply, place_reply).astype(BF)], axis=1
    )
    owned = lax.dynamic_slice_in_dim(ordering, place * SLOT, SLOT, 0)

    inner = layer_hidden(rows, *layer0[:3])
    blocks = to_tiles(dot(inner, layer0[3]).astype(BF)).reshape(dp, -1, LANES)
    share = blocks.shape[1]
    kept_tiles = lax.dynamic_slice_in_dim(to_tiles(rows), place * share, share, 0)
    next_tiles = (kept_tiles.astype(F32) + summed(blocks)).astype(BF)
    rows = from_tiles(spread(next_tiles, "dp"), width)

    slot_early = dot(owned, rows).astype(BF)
    inner = layer_hidden(rows, *layer1[:3])
    inner = dot(ordering, inner).astype(BF)
    blocks = dot(inner, layer1[3]).astype(BF).reshape(dp, SLOT, width)
    slot_late = (slot_early.astype(F32) + summed(blocks)).astype(BF)

    came = swap(jnp.where(first, slot_late, slot_early))
    kept = jnp.where(first, slot_early, slot_late)
    return jnp.where(first, jnp.stack([kept, came]), jnp.stack([came, kept]))[None]


def solution(mesh):
    placed = (
        P("section", "dp", None, "mp"),
        P("section", "dp"),
        P("section", "dp"),
        P("section", None),
        P("mp"),
        P("mp", "dp"),
        P("dp", "mp"),
        P("section", "mp"),
        P("section", "mp", "dp"),
        P("section", "mp", "dp"),
        P("section", "dp", "mp"),
    )
    return jax.shard_map(
        per_device,
        mesh=mesh,
        in_specs=placed,
        out_specs=P("section", None, "dp", "mp"),
        check_vma=False,
    )
```

```python
import jax
import jax.numpy as jnp
from jax import lax
from jax.sharding import PartitionSpec as P

D = 8192
VIS = 8192
MAXT = 2
TROWS = 2
LMAX = 4
IMG = MAXT * TROWS
SLOT = IMG + LMAX
EPS_LN = 1e-05
EPS_RMS = 1e-06
LANES = 128
DEAD = 64.0
BF = jnp.bfloat16
F32 = jnp.float32


def exchange(blocks, axis):
    return lax.all_to_all(blocks, axis, 0, 0, tiled=True)


def spread(block, axis):
    peers = lax.axis_size(axis)
    return exchange(jnp.broadcast_to(block[None], (peers,) + block.shape), axis)


def swap(block):
    return lax.ppermute(block, "section", [(0, 1), (1, 0)])


def terms(values, count):
    parts = []
    for _ in range(count):
        part = lax.reduce_precision(values, 8, 7)
        parts.append(part.astype(BF))
        values = values - part
    return parts


def dot(a, b):
    return jnp.dot(a, b, preferred_element_type=F32)


def marked(rows, count):
    alive = jnp.arange(rows.shape[0], dtype=jnp.int32) < count
    return jnp.where(alive[:, None], rows, jnp.asarray(DEAD, rows.dtype))


def placement(rows, key, kept):
    count = rows.shape[0]
    alive = jnp.broadcast_to((rows[:, :1] < DEAD / 2), (count, LANES)).astype(BF)
    before = (key[None, :] < key[:, None]).astype(BF)
    position = dot(before, alive)[:, :kept]
    at = lax.broadcasted_iota(jnp.int32, (count, kept), 1).astype(F32)
    return jnp.where(position == at, alive[:, :kept], jnp.asarray(0, BF))


def pick(matrix, rows):
    return lax.dot_general(
        matrix, rows, (((0,), (0,)), ((), ())), preferred_element_type=F32
    ).astype(BF)


def to_tiles(rows):
    count, width = rows.shape
    tiles = rows.reshape(count // 8, 8, width // LANES, LANES).transpose(0, 2, 1, 3)
    return tiles.reshape(-1, LANES)


def from_tiles(tiles, width):
    columns = width // LANES
    rows = tiles.reshape(-1, columns, 8, LANES).transpose(0, 2, 1, 3)
    return rows.reshape(-1, width)


def projector_partial(image, gain, w_in):
    width = image.shape[1]
    values = image.astype(F32)
    sums = jnp.sum(values, axis=1)
    squares = jnp.sum(values * values, axis=1)
    scaled = (values * gain.astype(F32)).astype(BF)
    column = dot(gain[None, :], w_in)
    centered = dot(scaled, w_in) - (sums / width)[:, None] * column
    rows, hidden = centered.shape
    small = jnp.stack(terms(sums, 3) + terms(squares, 3))
    small = jnp.pad(small, ((0, 0), (0, hidden - rows)))
    extra = jnp.concatenate([small, jnp.concatenate(terms(column, 3))], axis=0)
    extra = jnp.pad(extra, ((0, 16 - extra.shape[0]), (0, 0)))
    return jnp.concatenate([centered.astype(BF), extra], axis=0)


def projector_active(parts, rows, width):
    values = parts.astype(F32)
    extra = values[:, rows:]
    sums = jnp.sum(extra[:, 0:3, :rows], axis=1)
    squares = jnp.sum(extra[:, 3:6, :rows], axis=(0, 1))
    columns = jnp.sum(extra[:, 6:9], axis=1)
    center = jnp.sum(sums, axis=0) / VIS
    variance = squares / VIS - center * center
    offsets = sums / width - center[None, :]
    before = jnp.sum(values[:, :rows], axis=0)
    before = before + jnp.sum(offsets[:, :, None] * columns[:, None, :], axis=0)
    before = before * lax.rsqrt(variance + EPS_LN)[:, None]
    return jax.nn.gelu(before, approximate=False).astype(BF)


def layer_partial(rows, gain, w_gate, w_up):
    values = rows.astype(F32)
    squares = jnp.sum(values * values, axis=1)
    normed = (values * gain.astype(F32)).astype(BF)
    stats = jnp.pad(jnp.stack(terms(squares, 2), axis=1), ((0, 0), (0, LANES - 2)))
    return jnp.concatenate(
        [dot(normed, w_gate).astype(BF), dot(normed, w_up).astype(BF), stats], axis=1
    )


def layer_inner(parts, hidden):
    total = jnp.sum(parts.astype(F32), axis=0)
    squares = jnp.sum(total[:, 2 * hidden :], axis=1)
    factor = lax.rsqrt(squares / D + EPS_RMS)[:, None]
    gate_pre = total[:, :hidden] * factor
    up_pre = total[:, hidden : 2 * hidden] * factor
    return (jax.nn.silu(gate_pre) * up_pre).astype(BF)


def layer_hidden(rows, gain, w_gate, w_up):
    mp = lax.axis_size("mp")
    hidden = w_gate.shape[1]
    sent = layer_partial(rows, gain, w_gate, w_up)
    parts = exchange(sent.reshape(mp, rows.shape[0] // mp, -1), "mp")
    return spread(layer_inner(parts, hidden), "mp").reshape(rows.shape[0], hidden)


def summed(blocks):
    return jnp.sum(exchange(blocks, "dp").astype(F32), axis=0)


def per_device(
    rollout_rows,
    response_lengths,
    tile_counts,
    prompt_owner,
    proj_gain,
    proj_in,
    proj_out,
    norm_gain,
    gate_w,
    up_w,
    down_w,
):
    dp = lax.axis_size("dp")
    width = rollout_rows.shape[3]
    first = lax.axis_index("section") == 0
    place = lax.axis_index("dp")
    owners = prompt_owner[0]
    img_live = dp * TROWS * MAXT * 3 // 4
    local = rollout_rows[0, 0]
    local = jnp.concatenate(
        [
            marked(local[:IMG], tile_counts[0, 0] * TROWS),
            marked(local[IMG:], response_lengths[0, 0]),
        ]
    )
    copies = jnp.broadcast_to(local[None], (dp,) + local.shape)
    own = (norm_gain, gate_w[0], up_w[0], down_w[0])
    own, copies = lax.optimization_barrier((own, copies))
    other = tuple(swap(array) for array in own)
    layer0 = [jnp.where(first, a, b) for a, b in zip(own, other)]
    layer1 = [jnp.where(first, b, a) for a, b in zip(own, other)]
    layer0, layer1 = lax.optimization_barrier((layer0, layer1))
    layer0[0], layer1[0] = layer0[0][0], layer1[0][0]

    everyone = exchange(copies, "dp")
    gathered = everyone[:, :IMG].reshape(dp * IMG, width)
    replies = everyone[:, IMG:].reshape(dp * LMAX, width)

    index = jnp.arange(dp * IMG, dtype=jnp.int32)
    place_image = placement(gathered, index, img_live)
    image = pick(place_image, gathered)
    sent = projector_partial(image, proj_gain, proj_in)
    parts = spread(sent, "mp")
    active = projector_active(parts, img_live, width)
    blocks = to_tiles(dot(active, proj_out).astype(BF))
    projected = summed(blocks.reshape(dp, -1, LANES)).astype(BF)
    projected = from_tiles(spread(projected, "dp"), width)

    place_reply = placement(replies, index, img_live)
    rows = jnp.concatenate([projected, pick(place_reply, replies)], axis=0)

    slot_row = jnp.arange(dp * SLOT, dtype=jnp.int32)
    image_row = owners[:, None] * SLOT + jnp.arange(IMG, dtype=jnp.int32)[None, :]
    reply_row = owners[:, None] * SLOT + IMG + jnp.arange(LMAX, dtype=jnp.int32)[None, :]
    to_image = (slot_row[:, None] == image_row.reshape(-1)[None, :]).astype(BF)
    to_reply = (slot_row[:, None] == reply_row.reshape(-1)[None, :]).astype(BF)
    ordering = jnp.concatenate(
        [dot(to_image, place_image).astype(BF), dot(to_reply, place_reply).astype(BF)], axis=1
    )
    owned = lax.dynamic_slice_in_dim(ordering, place * SLOT, SLOT, 0)

    inner = layer_hidden(rows, *layer0[:3])
    blocks = to_tiles(dot(inner, layer0[3]).astype(BF)).reshape(dp, -1, LANES)
    share = blocks.shape[1]
    kept_tiles = lax.dynamic_slice_in_dim(to_tiles(rows), place * share, share, 0)
    next_tiles = (kept_tiles.astype(F32) + summed(blocks)).astype(BF)
    rows = from_tiles(spread(next_tiles, "dp"), width)

    slot_early = dot(owned, rows).astype(BF)
    inner = layer_hidden(rows, *layer1[:3])
    inner = dot(ordering, inner).astype(BF)
    blocks = dot(inner, layer1[3]).astype(BF).reshape(dp, SLOT, width)
    slot_late = (slot_early.astype(F32) + summed(blocks)).astype(BF)

    came = swap(jnp.where(first, slot_late, slot_early))
    kept = jnp.where(first, slot_early, slot_late)
    return jnp.where(first, jnp.stack([kept, came]), jnp.stack([came, kept]))[None]


def solution(mesh):
    placed = (
        P("section", "dp", None, "mp"),
        P("section", "dp"),
        P("section", "dp"),
        P("section", None),
        P("mp"),
        P("mp", "dp"),
        P("dp", "mp"),
        P("section", "mp"),
        P("section", "mp", "dp"),
        P("section", "mp", "dp"),
        P("section", "dp", "mp"),
    )
    return jax.shard_map(
        per_device,
        mesh=mesh,
        in_specs=placed,
        out_specs=P("section", None, "dp", "mp"),
        check_vma=False,
    )
```

```python
import jax
import jax.numpy as jnp
from jax import lax
from jax.sharding import PartitionSpec as P

D = 8192
VIS = 8192
MAXT = 2
TROWS = 2
LMAX = 4
IMG = MAXT * TROWS
SLOT = IMG + LMAX
EPS_LN = 1e-05
EPS_RMS = 1e-06
LANES = 128
DEAD = 64.0
BF = jnp.bfloat16
F32 = jnp.float32


def exchange(blocks, axis):
    return lax.all_to_all(blocks, axis, 0, 0, tiled=True)


def spread(block, axis):
    peers = lax.axis_size(axis)
    return exchange(jnp.broadcast_to(block[None], (peers,) + block.shape), axis)


def swap(block):
    return lax.ppermute(block, "section", [(0, 1), (1, 0)])


def terms(values, count):
    parts = []
    for _ in range(count):
        part = lax.reduce_precision(values, 8, 7)
        parts.append(part.astype(BF))
        values = values - part
    return parts


def dot(a, b):
    return jnp.dot(a, b, preferred_element_type=F32)


def marked(rows, count):
    alive = jnp.arange(rows.shape[0], dtype=jnp.int32) < count
    return jnp.where(alive[:, None], rows, jnp.asarray(DEAD, rows.dtype))


def placement(rows, key, kept):
    count = rows.shape[0]
    alive = jnp.broadcast_to((rows[:, :1] < DEAD / 2), (count, LANES)).astype(BF)
    before = (key[None, :] < key[:, None]).astype(BF)
    position = dot(before, alive)[:, :kept]
    at = lax.broadcasted_iota(jnp.int32, (count, kept), 1).astype(F32)
    return jnp.where(position == at, alive[:, :kept], jnp.asarray(0, BF))


def pick(matrix, rows):
    return lax.dot_general(
        matrix, rows, (((0,), (0,)), ((), ())), preferred_element_type=F32
    ).astype(BF)


def to_tiles(rows):
    count, width = rows.shape
    tiles = rows.reshape(count // 8, 8, width // LANES, LANES).transpose(0, 2, 1, 3)
    return tiles.reshape(-1, LANES)


def from_tiles(tiles, width):
    columns = width // LANES
    rows = tiles.reshape(-1, columns, 8, LANES).transpose(0, 2, 1, 3)
    return rows.reshape(-1, width)


def projector_partial(image, gain, w_in):
    width = image.shape[1]
    values = image.astype(F32)
    sums = jnp.sum(values, axis=1)
    squares = jnp.sum(values * values, axis=1)
    scaled = (values * gain.astype(F32)).astype(BF)
    column = dot(gain[None, :], w_in)
    centered = dot(scaled, w_in) - (sums / width)[:, None] * column
    rows, hidden = centered.shape
    small = jnp.stack(terms(sums, 3) + terms(squares, 3))
    small = jnp.pad(small, ((0, 0), (0, hidden - rows)))
    extra = jnp.concatenate([small, jnp.concatenate(terms(column, 3))], axis=0)
    extra = jnp.pad(extra, ((0, 16 - extra.shape[0]), (0, 0)))
    return jnp.concatenate([centered.astype(BF), extra], axis=0)


def projector_active(parts, rows, width):
    values = parts.astype(F32)
    extra = values[:, rows:]
    sums = jnp.sum(extra[:, 0:3, :rows], axis=1)
    squares = jnp.sum(extra[:, 3:6, :rows], axis=(0, 1))
    columns = jnp.sum(extra[:, 6:9], axis=1)
    center = jnp.sum(sums, axis=0) / VIS
    variance = squares / VIS - center * center
    offsets = sums / width - center[None, :]
    before = jnp.sum(values[:, :rows], axis=0)
    before = before + jnp.sum(offsets[:, :, None] * columns[:, None, :], axis=0)
    before = before * lax.rsqrt(variance + EPS_LN)[:, None]
    return jax.nn.gelu(before, approximate=False).astype(BF)


def layer_partial(rows, gain, w_gate, w_up):
    values = rows.astype(F32)
    squares = jnp.sum(values * values, axis=1)
    normed = (values * gain.astype(F32)).astype(BF)
    stats = jnp.pad(jnp.stack(terms(squares, 2), axis=1), ((0, 0), (0, LANES - 2)))
    return jnp.concatenate(
        [dot(normed, w_gate).astype(BF), dot(normed, w_up).astype(BF), stats], axis=1
    )


def layer_inner(parts, hidden):
    total = jnp.sum(parts.astype(F32), axis=0)
    squares = jnp.sum(total[:, 2 * hidden :], axis=1)
    factor = lax.rsqrt(squares / D + EPS_RMS)[:, None]
    gate_pre = total[:, :hidden] * factor
    up_pre = total[:, hidden : 2 * hidden] * factor
    return (jax.nn.silu(gate_pre) * up_pre).astype(BF)


def layer_hidden(rows, gain, w_gate, w_up):
    mp = lax.axis_size("mp")
    hidden = w_gate.shape[1]
    sent = layer_partial(rows, gain, w_gate, w_up)
    parts = exchange(sent.reshape(mp, rows.shape[0] // mp, -1), "mp")
    return spread(layer_inner(parts, hidden), "mp").reshape(rows.shape[0], hidden)


def summed(blocks):
    return jnp.sum(exchange(blocks, "dp").astype(F32), axis=0)


def per_device(
    rollout_rows,
    response_lengths,
    tile_counts,
    prompt_owner,
    proj_gain,
    proj_in,
    proj_out,
    norm_gain,
    gate_w,
    up_w,
    down_w,
):
    dp = lax.axis_size("dp")
    width = rollout_rows.shape[3]
    first = lax.axis_index("section") == 0
    place = lax.axis_index("dp")
    owners = prompt_owner[0]
    img_live = dp * TROWS * MAXT * 3 // 4
    local = rollout_rows[0, 0]
    local = jnp.concatenate(
        [
            marked(local[:IMG], tile_counts[0, 0] * TROWS),
            marked(local[IMG:], response_lengths[0, 0]),
        ]
    )
    copies = jnp.broadcast_to(local[None], (dp,) + local.shape)
    own = (norm_gain, gate_w[0], up_w[0], down_w[0])
    own, copies = lax.optimization_barrier((own, copies))
    other = tuple(swap(array) for array in own)
    everyone = exchange(copies, "dp")
    gathered = everyone[:, :IMG].reshape(dp * IMG, width)
    replies = everyone[:, IMG:].reshape(dp * LMAX, width)
    gathered, other = lax.optimization_barrier((gathered, other))
    layer0 = [jnp.where(first, a, b) for a, b in zip(own, other)]
    layer1 = [jnp.where(first, b, a) for a, b in zip(own, other)]
    layer0, layer1 = lax.optimization_barrier((layer0, layer1))
    layer0[0], layer1[0] = layer0[0][0], layer1[0][0]

    index = jnp.arange(dp * IMG, dtype=jnp.int32)
    place_image = placement(gathered, index, img_live)
    image = pick(place_image, gathered)
    sent = projector_partial(image, proj_gain, proj_in)
    parts = spread(sent, "mp")
    active = projector_active(parts, img_live, width)
    blocks = to_tiles(dot(active, proj_out).astype(BF))
    projected = summed(blocks.reshape(dp, -1, LANES)).astype(BF)
    projected = from_tiles(spread(projected, "dp"), width)

    place_reply = placement(replies, index, img_live)
    rows = jnp.concatenate([projected, pick(place_reply, replies)], axis=0)

    slot_row = jnp.arange(dp * SLOT, dtype=jnp.int32)
    image_row = owners[:, None] * SLOT + jnp.arange(IMG, dtype=jnp.int32)[None, :]
    reply_row = owners[:, None] * SLOT + IMG + jnp.arange(LMAX, dtype=jnp.int32)[None, :]
    to_image = (slot_row[:, None] == image_row.reshape(-1)[None, :]).astype(BF)
    to_reply = (slot_row[:, None] == reply_row.reshape(-1)[None, :]).astype(BF)
    ordering = jnp.concatenate(
        [dot(to_image, place_image).astype(BF), dot(to_reply, place_reply).astype(BF)], axis=1
    )
    owned = lax.dynamic_slice_in_dim(ordering, place * SLOT, SLOT, 0)

    gain0, gain1 = layer0[0].astype(F32), layer1[0].astype(F32)
    rows, ordering, owned, layer0, layer1, gain0, gain1 = lax.optimization_barrier(
        (rows, ordering, owned, layer0[1:], layer1[1:], gain0, gain1)
    )
    inner = layer_hidden(rows, gain0, *layer0[:2])
    blocks = to_tiles(dot(inner, layer0[2]).astype(BF)).reshape(dp, -1, LANES)
    total, rows = lax.optimization_barrier((exchange(blocks, "dp"), rows))
    share = total.shape[1]
    kept_tiles = lax.dynamic_slice_in_dim(to_tiles(rows), place * share, share, 0)
    next_tiles = (kept_tiles.astype(F32) + jnp.sum(total.astype(F32), axis=0)).astype(BF)
    rows = from_tiles(spread(next_tiles, "dp"), width)

    slot_early = dot(owned, rows).astype(BF)
    slot_early, rows = lax.optimization_barrier((slot_early, rows))
    inner = layer_hidden(rows, gain1, *layer1[:2])
    inner = dot(ordering, inner).astype(BF)
    blocks = dot(inner, layer1[2]).astype(BF).reshape(dp, SLOT, width)
    slot_late = (slot_early.astype(F32) + summed(blocks)).astype(BF)

    came = swap(jnp.where(first, slot_late, slot_early))
    kept = jnp.where(first, slot_early, slot_late)
    return jnp.where(first, jnp.stack([kept, came]), jnp.stack([came, kept]))[None]


def solution(mesh):
    placed = (
        P("section", "dp", None, "mp"),
        P("section", "dp"),
        P("section", "dp"),
        P("section", None),
        P("mp"),
        P("mp", "dp"),
        P("dp", "mp"),
        P("section", "mp"),
        P("section", "mp", "dp"),
        P("section", "mp", "dp"),
        P("section", "dp", "mp"),
    )
    return jax.shard_map(
        per_device,
        mesh=mesh,
        in_specs=placed,
        out_specs=P("section", None, "dp", "mp"),
        check_vma=False,
    )
```

```python
import jax
import jax.numpy as jnp
from jax import lax
from jax.sharding import PartitionSpec as P

D = 8192
VIS = 8192
MAXT = 2
TROWS = 2
LMAX = 4
IMG = MAXT * TROWS
SLOT = IMG + LMAX
EPS_LN = 1e-05
EPS_RMS = 1e-06
LANES = 128
DEAD = 64.0
BF = jnp.bfloat16
F32 = jnp.float32


def exchange(blocks, axis):
    peers = lax.axis_size(axis)
    order = None
    if axis == "mp":
        order = [list(range(0, peers, 2)) + list(range(1, peers, 2))]
    return lax.all_to_all(blocks, axis, 0, 0, tiled=True, axis_index_groups=order)


def spread(block, axis):
    peers = lax.axis_size(axis)
    return exchange(jnp.broadcast_to(block[None], (peers,) + block.shape), axis)


def swap(block):
    return lax.ppermute(block, "section", [(0, 1), (1, 0)])


def terms(values, count):
    parts = []
    for _ in range(count):
        part = lax.reduce_precision(values, 8, 7)
        parts.append(part.astype(BF))
        values = values - part
    return parts


def dot(a, b):
    return jnp.dot(a, b, preferred_element_type=F32)


def marked(rows, count):
    alive = jnp.arange(rows.shape[0], dtype=jnp.int32) < count
    return jnp.where(alive[:, None], rows, jnp.asarray(DEAD, rows.dtype))


def placement(rows, key, kept):
    count = rows.shape[0]
    alive = jnp.broadcast_to((rows[:, :1] < DEAD / 2), (count, LANES)).astype(BF)
    before = (key[None, :] < key[:, None]).astype(BF)
    position = dot(before, alive)[:, :kept]
    at = lax.broadcasted_iota(jnp.int32, (count, kept), 1).astype(F32)
    return jnp.where(position == at, alive[:, :kept], jnp.asarray(0, BF))


def pick(matrix, rows):
    return lax.dot_general(
        matrix, rows, (((0,), (0,)), ((), ())), preferred_element_type=F32
    ).astype(BF)


def to_tiles(rows):
    count, width = rows.shape
    tiles = rows.reshape(count // 8, 8, width // LANES, LANES).transpose(0, 2, 1, 3)
    return tiles.reshape(-1, LANES)


def from_tiles(tiles, width):
    columns = width // LANES
    rows = tiles.reshape(-1, columns, 8, LANES).transpose(0, 2, 1, 3)
    return rows.reshape(-1, width)


def projector_partial(image, gain, w_in):
    width = image.shape[1]
    values = image.astype(F32)
    sums = jnp.sum(values, axis=1)
    squares = jnp.sum(values * values, axis=1)
    scaled = (values * gain.astype(F32)).astype(BF)
    column = dot(gain[None, :], w_in)
    centered = dot(scaled, w_in) - (sums / width)[:, None] * column
    rows, hidden = centered.shape
    small = jnp.stack(terms(sums, 3) + terms(squares, 3))
    small = jnp.pad(small, ((0, 0), (0, hidden - rows)))
    extra = jnp.concatenate([small, jnp.concatenate(terms(column, 3))], axis=0)
    extra = jnp.pad(extra, ((0, 16 - extra.shape[0]), (0, 0)))
    return jnp.concatenate([centered.astype(BF), extra], axis=0)


def projector_active(parts, rows, width):
    values = parts.astype(F32)
    extra = values[:, rows:]
    sums = jnp.sum(extra[:, 0:3, :rows], axis=1)
    squares = jnp.sum(extra[:, 3:6, :rows], axis=(0, 1))
    columns = jnp.sum(extra[:, 6:9], axis=1)
    center = jnp.sum(sums, axis=0) / VIS
    variance = squares / VIS - center * center
    offsets = sums / width - center[None, :]
    before = jnp.sum(values[:, :rows], axis=0)
    before = before + jnp.sum(offsets[:, :, None] * columns[:, None, :], axis=0)
    before = before * lax.rsqrt(variance + EPS_LN)[:, None]
    return jax.nn.gelu(before, approximate=False).astype(BF)


def layer_partial(rows, gain, w_gate, w_up):
    values = rows.astype(F32)
    squares = jnp.sum(values * values, axis=1)
    normed = (values * gain.astype(F32)).astype(BF)
    stats = jnp.pad(jnp.stack(terms(squares, 2), axis=1), ((0, 0), (0, LANES - 2)))
    return jnp.concatenate(
        [dot(normed, w_gate).astype(BF), dot(normed, w_up).astype(BF), stats], axis=1
    )


def layer_inner(parts, hidden):
    total = jnp.sum(parts.astype(F32), axis=0)
    squares = jnp.sum(total[:, 2 * hidden :], axis=1)
    factor = lax.rsqrt(squares / D + EPS_RMS)[:, None]
    gate_pre = total[:, :hidden] * factor
    up_pre = total[:, hidden : 2 * hidden] * factor
    return (jax.nn.silu(gate_pre) * up_pre).astype(BF)


def layer_hidden(rows, gain, w_gate, w_up):
    mp = lax.axis_size("mp")
    hidden = w_gate.shape[1]
    sent = layer_partial(rows, gain, w_gate, w_up)
    parts = exchange(sent.reshape(mp, rows.shape[0] // mp, -1), "mp")
    return spread(layer_inner(parts, hidden), "mp").reshape(rows.shape[0], hidden)


def summed(blocks):
    return jnp.sum(exchange(blocks, "dp").astype(F32), axis=0)


def per_device(
    rollout_rows,
    response_lengths,
    tile_counts,
    prompt_owner,
    proj_gain,
    proj_in,
    proj_out,
    norm_gain,
    gate_w,
    up_w,
    down_w,
):
    dp = lax.axis_size("dp")
    width = rollout_rows.shape[3]
    first = lax.axis_index("section") == 0
    place = lax.axis_index("dp")
    owners = prompt_owner[0]
    img_live = dp * TROWS * MAXT * 3 // 4
    local = rollout_rows[0, 0]
    local = jnp.concatenate(
        [
            marked(local[:IMG], tile_counts[0, 0] * TROWS),
            marked(local[IMG:], response_lengths[0, 0]),
        ]
    )
    copies = jnp.broadcast_to(local[None], (dp,) + local.shape)
    own = (norm_gain, gate_w[0], up_w[0], down_w[0])
    own, copies = lax.optimization_barrier((own, copies))
    other = tuple(swap(array) for array in own)
    everyone = exchange(copies, "dp")
    gathered = everyone[:, :IMG].reshape(dp * IMG, width)
    replies = everyone[:, IMG:].reshape(dp * LMAX, width)
    gathered, other = lax.optimization_barrier((gathered, other))
    layer0 = [jnp.where(first, a, b) for a, b in zip(own[1:], other[1:])]
    layer1 = [jnp.where(first, b, a) for a, b in zip(own[1:], other[1:])]
    layer0, layer1 = lax.optimization_barrier((layer0, layer1))

    index = jnp.arange(dp * IMG, dtype=jnp.int32)
    place_image = placement(gathered, index, img_live)
    image = pick(place_image, gathered)
    sent = projector_partial(image, proj_gain, proj_in)
    parts = spread(sent, "mp")
    active = projector_active(parts, img_live, width)
    blocks = to_tiles(dot(active, proj_out).astype(BF))
    projected = summed(blocks.reshape(dp, -1, LANES)).astype(BF)
    projected = from_tiles(spread(projected, "dp"), width)

    place_reply = placement(replies, index, img_live)
    rows = jnp.concatenate([projected, pick(place_reply, replies)], axis=0)

    slot_row = jnp.arange(dp * SLOT, dtype=jnp.int32)
    image_row = owners[:, None] * SLOT + jnp.arange(IMG, dtype=jnp.int32)[None, :]
    reply_row = owners[:, None] * SLOT + IMG + jnp.arange(LMAX, dtype=jnp.int32)[None, :]
    to_image = (slot_row[:, None] == image_row.reshape(-1)[None, :]).astype(BF)
    to_reply = (slot_row[:, None] == reply_row.reshape(-1)[None, :]).astype(BF)
    ordering = jnp.concatenate(
        [dot(to_image, place_image).astype(BF), dot(to_reply, place_reply).astype(BF)], axis=1
    )
    owned = lax.dynamic_slice_in_dim(ordering, place * SLOT, SLOT, 0)

    rows, ordering, owned, layer0, layer1, gains = lax.optimization_barrier(
        (rows, ordering, owned, layer0, layer1, (own[0], other[0]))
    )
    gain0 = jnp.where(first, *gains)[0].astype(F32)
    inner = layer_hidden(rows, gain0, *layer0[:2])
    blocks = to_tiles(dot(inner, layer0[2]).astype(BF)).reshape(dp, -1, LANES)
    total, rows, at = lax.optimization_barrier((exchange(blocks, "dp"), rows, place))
    share = total.shape[1]
    kept_tiles = lax.dynamic_slice_in_dim(to_tiles(rows), at * share, share, 0)
    next_tiles = (kept_tiles.astype(F32) + jnp.sum(total.astype(F32), axis=0)).astype(BF)
    rows = from_tiles(spread(next_tiles, "dp"), width)

    slot_early = dot(owned, rows).astype(BF)
    slot_early, rows, gains = lax.optimization_barrier((slot_early, rows, gains))
    gain1 = jnp.where(first, *gains[::-1])[0].astype(F32)
    inner = layer_hidden(rows, gain1, *layer1[:2])
    inner = dot(ordering, inner).astype(BF)
    blocks = dot(inner, layer1[2]).astype(BF).reshape(dp, SLOT, width)
    slot_late = (slot_early.astype(F32) + summed(blocks)).astype(BF)

    came = swap(jnp.where(first, slot_late, slot_early))
    kept = jnp.where(first, slot_early, slot_late)
    return jnp.where(first, jnp.stack([kept, came]), jnp.stack([came, kept]))[None]


def solution(mesh):
    placed = (
        P("section", "dp", None, "mp"),
        P("section", "dp"),
        P("section", "dp"),
        P("section", None),
        P("mp"),
        P("mp", "dp"),
        P("dp", "mp"),
        P("section", "mp"),
        P("section", "mp", "dp"),
        P("section", "mp", "dp"),
        P("section", "dp", "mp"),
    )
    return jax.shard_map(
        per_device,
        mesh=mesh,
        in_specs=placed,
        out_specs=P("section", None, "dp", "mp"),
        check_vma=False,
    )
```

```python
import jax
import jax.numpy as jnp
from jax import lax
from jax.sharding import PartitionSpec as P

D = 8192
VIS = 8192
MAXT = 2
TROWS = 2
LMAX = 4
IMG = MAXT * TROWS
SLOT = IMG + LMAX
EPS_LN = 1e-05
EPS_RMS = 1e-06
LANES = 128
DEAD = 64.0
BF = jnp.bfloat16
F32 = jnp.float32


def exchange(blocks, axis):
    peers = lax.axis_size(axis)
    order = None
    if axis == "mp":
        order = [[0, 1, 4, 5, 2, 3, 6, 7]]
    return lax.all_to_all(blocks, axis, 0, 0, tiled=True, axis_index_groups=order)


def spread(block, axis):
    peers = lax.axis_size(axis)
    return exchange(jnp.broadcast_to(block[None], (peers,) + block.shape), axis)


def swap(block):
    return lax.ppermute(block, "section", [(0, 1), (1, 0)])


def terms(values, count):
    parts = []
    for _ in range(count):
        part = lax.reduce_precision(values, 8, 7)
        parts.append(part.astype(BF))
        values = values - part
    return parts


def dot(a, b):
    return jnp.dot(a, b, preferred_element_type=F32)


def marked(rows, count):
    alive = jnp.arange(rows.shape[0], dtype=jnp.int32) < count
    return jnp.where(alive[:, None], rows, jnp.asarray(DEAD, rows.dtype))


def placement(rows, key, kept):
    count = rows.shape[0]
    alive = jnp.broadcast_to((rows[:, :1] < DEAD / 2), (count, LANES)).astype(BF)
    before = (key[None, :] < key[:, None]).astype(BF)
    position = dot(before, alive)[:, :kept]
    at = lax.broadcasted_iota(jnp.int32, (count, kept), 1).astype(F32)
    return jnp.where(position == at, alive[:, :kept], jnp.asarray(0, BF))


def pick(matrix, rows):
    return lax.dot_general(
        matrix, rows, (((0,), (0,)), ((), ())), preferred_element_type=F32
    ).astype(BF)


def to_tiles(rows):
    count, width = rows.shape
    tiles = rows.reshape(count // 8, 8, width // LANES, LANES).transpose(0, 2, 1, 3)
    return tiles.reshape(-1, LANES)


def from_tiles(tiles, width):
    columns = width // LANES
    rows = tiles.reshape(-1, columns, 8, LANES).transpose(0, 2, 1, 3)
    return rows.reshape(-1, width)


def projector_partial(image, gain, w_in):
    width = image.shape[1]
    values = image.astype(F32)
    sums = jnp.sum(values, axis=1)
    squares = jnp.sum(values * values, axis=1)
    scaled = (values * gain.astype(F32)).astype(BF)
    column = dot(gain[None, :], w_in)
    centered = dot(scaled, w_in) - (sums / width)[:, None] * column
    rows, hidden = centered.shape
    small = jnp.stack(terms(sums, 3) + terms(squares, 3))
    small = jnp.pad(small, ((0, 0), (0, hidden - rows)))
    extra = jnp.concatenate([small, jnp.concatenate(terms(column, 3))], axis=0)
    extra = jnp.pad(extra, ((0, 16 - extra.shape[0]), (0, 0)))
    return jnp.concatenate([centered.astype(BF), extra], axis=0)


def projector_active(parts, rows, width):
    values = parts.astype(F32)
    extra = values[:, rows:]
    sums = jnp.sum(extra[:, 0:3, :rows], axis=1)
    squares = jnp.sum(extra[:, 3:6, :rows], axis=(0, 1))
    columns = jnp.sum(extra[:, 6:9], axis=1)
    center = jnp.sum(sums, axis=0) / VIS
    variance = squares / VIS - center * center
    offsets = sums / width - center[None, :]
    before = jnp.sum(values[:, :rows], axis=0)
    before = before + jnp.sum(offsets[:, :, None] * columns[:, None, :], axis=0)
    before = before * lax.rsqrt(variance + EPS_LN)[:, None]
    return jax.nn.gelu(before, approximate=False).astype(BF)


def layer_partial(rows, gain, w_gate, w_up):
    values = rows.astype(F32)
    squares = jnp.sum(values * values, axis=1, keepdims=True)
    normed = (values * gain.astype(F32)).astype(BF)
    coarse = lax.reduce_precision(squares, 8, 7)
    lane = lax.broadcasted_iota(jnp.int32, (rows.shape[0], LANES), 1)
    stats = jnp.where(lane == 0, coarse, jnp.where(lane == 1, squares - coarse, 0)).astype(BF)
    return jnp.concatenate(
        [dot(normed, w_gate).astype(BF), dot(normed, w_up).astype(BF), stats], axis=1
    )


def layer_inner(parts, hidden):
    total = jnp.sum(parts.astype(F32), axis=0)
    squares = jnp.sum(total[:, 2 * hidden :], axis=1)
    factor = lax.rsqrt(squares / D + EPS_RMS)[:, None]
    gate_pre = total[:, :hidden] * factor
    up_pre = total[:, hidden : 2 * hidden] * factor
    return (jax.nn.silu(gate_pre) * up_pre).astype(BF)


def layer_hidden(rows, gain, w_gate, w_up):
    mp = lax.axis_size("mp")
    hidden = w_gate.shape[1]
    sent = layer_partial(rows, gain, w_gate, w_up)
    parts = exchange(sent.reshape(mp, rows.shape[0] // mp, -1), "mp")
    return spread(layer_inner(parts, hidden), "mp").reshape(rows.shape[0], hidden)


def summed(blocks):
    return jnp.sum(exchange(blocks, "dp").astype(F32), axis=0)


def per_device(
    rollout_rows,
    response_lengths,
    tile_counts,
    prompt_owner,
    proj_gain,
    proj_in,
    proj_out,
    norm_gain,
    gate_w,
    up_w,
    down_w,
):
    dp = lax.axis_size("dp")
    width = rollout_rows.shape[3]
    first = lax.axis_index("section") == 0
    place = lax.axis_index("dp")
    owners = prompt_owner[0]
    img_live = dp * TROWS * MAXT * 3 // 4
    local = rollout_rows[0, 0]
    local = jnp.concatenate(
        [
            marked(local[:IMG], tile_counts[0, 0] * TROWS),
            marked(local[IMG:], response_lengths[0, 0]),
        ]
    )
    copies = jnp.broadcast_to(local[None], (dp,) + local.shape)
    own = (norm_gain, gate_w[0], up_w[0], down_w[0])
    own, copies = lax.optimization_barrier((own, copies))
    other = tuple(swap(array) for array in own)
    everyone = exchange(copies, "dp")
    gathered = everyone[:, :IMG].reshape(dp * IMG, width)
    replies = everyone[:, IMG:].reshape(dp * LMAX, width)
    gathered, other = lax.optimization_barrier((gathered, other))
    layer0 = [jnp.where(first, a, b) for a, b in zip(own[1:], other[1:])]
    layer1 = [jnp.where(first, b, a) for a, b in zip(own[1:], other[1:])]
    layer0, layer1 = lax.optimization_barrier((layer0, layer1))

    index = jnp.arange(dp * IMG, dtype=jnp.int32)
    place_image = placement(gathered, index, img_live)
    image = pick(place_image, gathered)
    sent = projector_partial(image, proj_gain, proj_in)
    sent, everyone = lax.optimization_barrier((sent, everyone))
    parts = spread(sent, "mp")
    replies = everyone[:, IMG:].reshape(dp * LMAX, width)
    active = projector_active(parts, img_live, width)
    blocks = to_tiles(dot(active, proj_out).astype(BF))
    projected = summed(blocks.reshape(dp, -1, LANES)).astype(BF)
    projected = from_tiles(spread(projected, "dp"), width)

    place_reply = placement(replies, index, img_live)
    rows = jnp.concatenate([projected, pick(place_reply, replies)], axis=0)

    slot_row = jnp.arange(dp * SLOT, dtype=jnp.int32)
    image_row = owners[:, None] * SLOT + jnp.arange(IMG, dtype=jnp.int32)[None, :]
    reply_row = owners[:, None] * SLOT + IMG + jnp.arange(LMAX, dtype=jnp.int32)[None, :]
    to_image = (slot_row[:, None] == image_row.reshape(-1)[None, :]).astype(BF)
    to_reply = (slot_row[:, None] == reply_row.reshape(-1)[None, :]).astype(BF)
    ordering = jnp.concatenate(
        [dot(to_image, place_image).astype(BF), dot(to_reply, place_reply).astype(BF)], axis=1
    )
    owned = lax.dynamic_slice_in_dim(ordering, place * SLOT, SLOT, 0)

    rows, ordering, owned, layer0, layer1, gains = lax.optimization_barrier(
        (rows, ordering, owned, layer0, layer1, (own[0], other[0]))
    )
    gain0 = jnp.where(first, *gains)[0].astype(F32)
    inner = layer_hidden(rows, gain0, *layer0[:2])
    blocks = to_tiles(dot(inner, layer0[2]).astype(BF)).reshape(dp, -1, LANES)
    total, rows, at = lax.optimization_barrier((exchange(blocks, "dp"), rows, place))
    share = total.shape[1]
    kept_tiles = lax.dynamic_slice_in_dim(to_tiles(rows), at * share, share, 0)
    next_tiles = (kept_tiles.astype(F32) + jnp.sum(total.astype(F32), axis=0)).astype(BF)
    rows = from_tiles(spread(next_tiles, "dp"), width)

    slot_early = dot(owned, rows).astype(BF)
    slot_early, rows, gains = lax.optimization_barrier((slot_early, rows, gains))
    gain1 = jnp.where(first, *gains[::-1])[0].astype(F32)
    inner = layer_hidden(rows, gain1, *layer1[:2])
    inner = dot(ordering, inner).astype(BF)
    blocks = dot(inner, layer1[2]).astype(BF).reshape(dp, SLOT, width)
    slot_late = (slot_early.astype(F32) + summed(blocks)).astype(BF)

    came = swap(jnp.where(first, slot_late, slot_early))
    kept = jnp.where(first, slot_early, slot_late)
    return jnp.where(first, jnp.stack([kept, came]), jnp.stack([came, kept]))[None]


def solution(mesh):
    placed = (
        P("section", "dp", None, "mp"),
        P("section", "dp"),
        P("section", "dp"),
        P("section", None),
        P("mp"),
        P("mp", "dp"),
        P("dp", "mp"),
        P("section", "mp"),
        P("section", "mp", "dp"),
        P("section", "mp", "dp"),
        P("section", "dp", "mp"),
    )
    return jax.shard_map(
        per_device,
        mesh=mesh,
        in_specs=placed,
        out_specs=P("section", None, "dp", "mp"),
        check_vma=False,
    )
```

```python
import jax
import jax.numpy as jnp
from jax import lax
from jax.sharding import PartitionSpec as P

D = 8192
VIS = 8192
MAXT = 2
TROWS = 2
LMAX = 4
IMG = MAXT * TROWS
SLOT = IMG + LMAX
EPS_LN = 1e-05
EPS_RMS = 1e-06
LANES = 128
DEAD = 64.0
BF = jnp.bfloat16
F32 = jnp.float32


def exchange(blocks, axis):
    peers = lax.axis_size(axis)
    order = None
    if axis == "mp":
        order = [[0, 1, 4, 5, 2, 3, 6, 7]]
    return lax.all_to_all(blocks, axis, 0, 0, tiled=True, axis_index_groups=order)


def spread(block, axis):
    peers = lax.axis_size(axis)
    return exchange(jnp.broadcast_to(block[None], (peers,) + block.shape), axis)


def swap(block):
    return lax.ppermute(block, "section", [(0, 1), (1, 0)])


def terms(values, count):
    parts = []
    for _ in range(count):
        part = lax.reduce_precision(values, 8, 7)
        parts.append(part.astype(BF))
        values = values - part
    return parts


def dot(a, b):
    return jnp.dot(a, b, preferred_element_type=F32)


def marked(rows, count):
    alive = jnp.arange(rows.shape[0], dtype=jnp.int32) < count
    return jnp.where(alive[:, None], rows, jnp.asarray(DEAD, rows.dtype))


def placement(rows, key, kept):
    count = rows.shape[0]
    alive = jnp.broadcast_to((rows[:, :1] < DEAD / 2), (count, LANES)).astype(BF)
    before = (key[None, :] < key[:, None]).astype(BF)
    position = dot(before, alive)[:, :kept]
    at = lax.broadcasted_iota(jnp.int32, (count, kept), 1).astype(F32)
    return jnp.where(position == at, alive[:, :kept], jnp.asarray(0, BF))


def pick(matrix, rows):
    return lax.dot_general(
        matrix, rows, (((0,), (0,)), ((), ())), preferred_element_type=F32
    ).astype(BF)


def to_tiles(rows):
    count, width = rows.shape
    tiles = rows.reshape(count // 8, 8, width // LANES, LANES).transpose(0, 2, 1, 3)
    return tiles.reshape(-1, LANES)


def from_tiles(tiles, width):
    columns = width // LANES
    rows = tiles.reshape(-1, columns, 8, LANES).transpose(0, 2, 1, 3)
    return rows.reshape(-1, width)


def projector_partial(image, gain, w_in):
    width = image.shape[1]
    values = image.astype(F32)
    sums = jnp.sum(values, axis=1)
    squares = jnp.sum(values * values, axis=1)
    scaled = (values * gain.astype(F32)).astype(BF)
    column = dot(gain[None, :], w_in)
    centered = dot(scaled, w_in) - (sums / width)[:, None] * column
    rows, hidden = centered.shape
    half = hidden // 2
    spare = ((0, 0), (0, half - rows))
    small = jnp.concatenate(
        [jnp.pad(jnp.stack(terms(values, 3)), spare) for values in (sums, squares)], axis=1
    )
    extra = jnp.concatenate([small, jnp.concatenate(terms(column, 3))], axis=0)
    extra = jnp.pad(extra, ((0, 8 - extra.shape[0]), (0, 0)))
    return jnp.concatenate([centered.astype(BF), extra], axis=0)


def projector_active(parts, rows, width):
    values = parts.astype(F32)
    extra = values[:, rows:]
    sums = jnp.sum(extra[:, 0:3, :rows], axis=1)
    half = extra.shape[2] // 2
    squares = jnp.sum(extra[:, 0:3, half : half + rows], axis=(0, 1))
    columns = jnp.sum(extra[:, 3:6], axis=1)
    center = jnp.sum(sums, axis=0) / VIS
    variance = squares / VIS - center * center
    offsets = sums / width - center[None, :]
    before = jnp.sum(values[:, :rows], axis=0)
    before = before + jnp.sum(offsets[:, :, None] * columns[:, None, :], axis=0)
    before = before * lax.rsqrt(variance + EPS_LN)[:, None]
    return jax.nn.gelu(before, approximate=False).astype(BF)


def layer_partial(rows, gain, w_gate, w_up):
    values = rows.astype(F32)
    squares = jnp.sum(values * values, axis=1, keepdims=True)
    normed = (values * gain.astype(F32)).astype(BF)
    coarse = lax.reduce_precision(squares, 8, 7)
    lane = lax.broadcasted_iota(jnp.int32, (rows.shape[0], LANES), 1)
    stats = jnp.where(lane == 0, coarse, jnp.where(lane == 1, squares - coarse, 0)).astype(BF)
    return jnp.concatenate(
        [dot(normed, w_gate).astype(BF), dot(normed, w_up).astype(BF), stats], axis=1
    )


def layer_inner(parts, hidden):
    total = jnp.sum(parts.astype(F32), axis=0)
    squares = jnp.sum(total[:, 2 * hidden :], axis=1)
    factor = lax.rsqrt(squares / D + EPS_RMS)[:, None]
    gate_pre = total[:, :hidden] * factor
    up_pre = total[:, hidden : 2 * hidden] * factor
    return (jax.nn.silu(gate_pre) * up_pre).astype(BF)


def layer_hidden(rows, gain, w_gate, w_up):
    mp = lax.axis_size("mp")
    hidden = w_gate.shape[1]
    sent = layer_partial(rows, gain, w_gate, w_up)
    parts = exchange(sent.reshape(mp, rows.shape[0] // mp, -1), "mp")
    return spread(layer_inner(parts, hidden), "mp").reshape(rows.shape[0], hidden)


def summed(blocks):
    return jnp.sum(exchange(blocks, "dp").astype(F32), axis=0)


def per_device(
    rollout_rows,
    response_lengths,
    tile_counts,
    prompt_owner,
    proj_gain,
    proj_in,
    proj_out,
    norm_gain,
    gate_w,
    up_w,
    down_w,
):
    dp = lax.axis_size("dp")
    width = rollout_rows.shape[3]
    first = lax.axis_index("section") == 0
    place = lax.axis_index("dp")
    owners = prompt_owner[0]
    img_live = dp * TROWS * MAXT * 3 // 4
    local = rollout_rows[0, 0]
    local = jnp.concatenate(
        [
            marked(local[:IMG], tile_counts[0, 0] * TROWS),
            marked(local[IMG:], response_lengths[0, 0]),
        ]
    )
    copies = jnp.broadcast_to(local[None], (dp,) + local.shape)
    own = (norm_gain, gate_w[0], up_w[0], down_w[0])
    own, copies = lax.optimization_barrier((own, copies))
    other = tuple(swap(array) for array in own)
    everyone = exchange(copies, "dp")
    gathered = everyone[:, :IMG].reshape(dp * IMG, width)
    replies = everyone[:, IMG:].reshape(dp * LMAX, width)
    gathered, other = lax.optimization_barrier((gathered, other))
    layer0 = [jnp.where(first, a, b) for a, b in zip(own[1:], other[1:])]
    layer1 = [jnp.where(first, b, a) for a, b in zip(own[1:], other[1:])]
    layer0, layer1 = lax.optimization_barrier((layer0, layer1))

    index = jnp.arange(dp * IMG, dtype=jnp.int32)
    place_image = placement(gathered, index, img_live)
    image = pick(place_image, gathered)
    sent = projector_partial(image, proj_gain, proj_in)
    sent, everyone = lax.optimization_barrier((sent, everyone))
    parts = spread(sent, "mp")
    replies = everyone[:, IMG:].reshape(dp * LMAX, width)
    active = projector_active(parts, img_live, width)
    blocks = to_tiles(dot(active, proj_out).astype(BF))
    projected = summed(blocks.reshape(dp, -1, LANES)).astype(BF)
    projected = from_tiles(spread(projected, "dp"), width)

    place_reply = placement(replies, index, img_live)
    rows = jnp.concatenate([projected, pick(place_reply, replies)], axis=0)

    slot_row = jnp.arange(dp * SLOT, dtype=jnp.int32)
    image_row = owners[:, None] * SLOT + jnp.arange(IMG, dtype=jnp.int32)[None, :]
    reply_row = owners[:, None] * SLOT + IMG + jnp.arange(LMAX, dtype=jnp.int32)[None, :]
    to_image = (slot_row[:, None] == image_row.reshape(-1)[None, :]).astype(BF)
    to_reply = (slot_row[:, None] == reply_row.reshape(-1)[None, :]).astype(BF)
    ordering = jnp.concatenate(
        [dot(to_image, place_image).astype(BF), dot(to_reply, place_reply).astype(BF)], axis=1
    )
    owned = lax.dynamic_slice_in_dim(ordering, place * SLOT, SLOT, 0)

    rows, ordering, owned, layer0, layer1, gains = lax.optimization_barrier(
        (rows, ordering, owned, layer0, layer1, (own[0], other[0]))
    )
    gain0 = jnp.where(first, *gains)[0].astype(F32)
    inner = layer_hidden(rows, gain0, *layer0[:2])
    blocks = to_tiles(dot(inner, layer0[2]).astype(BF)).reshape(dp, -1, LANES)
    total, rows, at = lax.optimization_barrier((exchange(blocks, "dp"), rows, place))
    share = total.shape[1]
    kept_tiles = lax.dynamic_slice_in_dim(to_tiles(rows), at * share, share, 0)
    next_tiles = (kept_tiles.astype(F32) + jnp.sum(total.astype(F32), axis=0)).astype(BF)
    rows = from_tiles(spread(next_tiles, "dp"), width)

    slot_early = dot(owned, rows).astype(BF)
    slot_early, rows, gains = lax.optimization_barrier((slot_early, rows, gains))
    gain1 = jnp.where(first, *gains[::-1])[0].astype(F32)
    inner = layer_hidden(rows, gain1, *layer1[:2])
    inner = dot(ordering, inner).astype(BF)
    blocks = dot(inner, layer1[2]).astype(BF).reshape(dp, SLOT, width)
    slot_late = (slot_early.astype(F32) + summed(blocks)).astype(BF)

    came = swap(jnp.where(first, slot_late, slot_early))
    kept = jnp.where(first, slot_early, slot_late)
    return jnp.where(first, jnp.stack([kept, came]), jnp.stack([came, kept]))[None]


def solution(mesh):
    placed = (
        P("section", "dp", None, "mp"),
        P("section", "dp"),
        P("section", "dp"),
        P("section", None),
        P("mp"),
        P("mp", "dp"),
        P("dp", "mp"),
        P("section", "mp"),
        P("section", "mp", "dp"),
        P("section", "mp", "dp"),
        P("section", "dp", "mp"),
    )
    return jax.shard_map(
        per_device,
        mesh=mesh,
        in_specs=placed,
        out_specs=P("section", None, "dp", "mp"),
        check_vma=False,
    )
```
